32 devices in a mesh: groups: 2 (over x), box: 16 (over z, y, core).
Axes of the slice: x: 2, y: 2, z: 4, core: 2. Of those that a mesh axis runs over, the one named last changes fastest.
Arguments:
- currents: bfloat16 [2048, 2, 128], P(('groups', 'box')), parts along dimension 0, may hold values from -6 to 6
- near_blocks: bfloat16 [1024, 4, 2, 128, 128], P('box'), may hold values from -0.1875 to 0.1875
- near_off: int32 [1024, 4], P('box'), may hold values from -32 to 32, as said below
- radiation: bfloat16 [1024, 2, 128, 128], P('box'), may hold values from -0.375 to 0.375
- interp: bfloat16 [512, 128], replicated, may hold values from -0.5 to 0.5
- translators: float32 [316, 2, 512], replicated, may hold values from -0.3125 to 0.3125
- send_list: int32 [16, 16, 16], P('box'), may hold values from 0 to 63
- inter_slot: int32 [1024, 189], P('box'), may hold values from 0 to 255, as said below
- trans_id: int32 [1024, 189], P('box'), may hold values from 0 to 315
Outputs:
- product: bfloat16 [2048, 2, 128], P(('groups', 'box')), parts along dimension 0
The draws below stay inside these ranges and needn't reach their ends.
There are 2 independent parts, one for each index of `groups`. The reference program is written for one: setup_inputs(seed, part) draws one part's arguments, and reference() takes and returns one part's arrays. A program takes and returns all parts, laid end to end along the dimension named above; an argument that names none is the same for every part. Nothing has to cross between parts.
Inputs may be any that keep to these rules, and one draw needn't show every extreme that they name: `near_off`: entry 0 of every box is 0 (its own block); offsets reach -32 and 32 on every device. `inter_slot`: each entry's sender lies within 3 device indices of the box's own device; slots from one such sender to one receiver are used up to a count of 1 to 16, slots from farther devices never; all 16 from a device to itself, and entry 0 of each box is a slot of its own device.
All inputs are finite; a program needn't handle non-finite values.
Results may differ from the reference program's by a relative error of at most 0.007.
Values may be sent and summed in bfloat16 or wider, within the bound.
A program may use at most 128 MiB of HBM per device.

```python
import jax
import jax.numpy as jnp
from jax import lax

M = 128
P_SIZE = 512
Q = 128
NB = 4
K = 189
NT = 316
BOX_DEV = 64
CAP = 16
BOXES = 1024
N_BOX = 16


def draw_near_off(key, part):
    key = jax.random.fold_in(key, 11)
    first, second = jax.random.split(key)
    rim_width = BOX_DEV // 2
    magnitude = jax.random.randint(first, (BOXES, NB), 1, rim_width + 1)
    signs = jax.random.randint(second, (BOXES, NB), 0, 2) * 2 - 1
    offsets = magnitude * signs
    rows = jnp.arange(BOXES, dtype=jnp.int32) % BOX_DEV
    column = jnp.arange(NB, dtype=jnp.int32)
    offsets = jnp.where(column[None, :] == 0, 0, offsets)
    offsets = jnp.where((column[None, :] == 1) & (rows[:, None] == 0), 0 - rim_width, offsets)
    offsets = jnp.where((column[None, :] == 1) & (rows[:, None] == BOX_DEV - 1), rim_width, offsets)
    return offsets.astype(jnp.int32)


def draw_inter_slot(key, part):
    key = jax.random.fold_in(key, 23)
    first, second, third, fourth = jax.random.split(key, 4)
    peer_count = BOXES // BOX_DEV
    counts = jax.random.randint(first, (peer_count, peer_count), 1, CAP + 1)
    counts = jnp.where(jnp.eye(peer_count, dtype=jnp.int32) == 1, CAP, counts)
    box_index = jnp.arange(BOXES, dtype=jnp.int32)
    owners = box_index // BOX_DEV
    distance = jax.random.randint(second, (BOXES, K), -3, 4) * jax.random.randint(fourth, (BOXES, K), 0, 2)
    senders = owners[:, None] + distance
    senders = jnp.where((senders < 0) | (senders >= peer_count), owners[:, None] - distance, senders)
    live = counts[senders, owners[:, None]]
    within = jax.random.randint(third, (BOXES, K), 0, live)
    slots = senders * CAP + within
    own_slot = owners * CAP + box_index % BOX_DEV % CAP
    slots = slots.at[:, 0].set(own_slot)
    return slots.astype(jnp.int32)


def touch_ends(drawn, own_key, least, top_value):
    shape = drawn.shape
    place = [jax.random.randint(jax.random.fold_in(own_key, axis), (), 0, shape[axis]) for axis in range(len(shape))]
    drawn = drawn.at[tuple(place)].set(least)
    longest = shape.index(max(shape))
    place[longest] = (place[longest] + 1) % shape[longest]
    return drawn.at[tuple(place)].set(top_value)


def steps_of(own_key, shape, cuts, low, high):
    loudness, own = 1.0, jax.random.fold_in(own_key, 6)
    for dim, blocks in cuts:
        draws = jnp.exp(jax.random.uniform(jax.random.fold_in(own, dim), (blocks,), jnp.float32, low / len(cuts), high / len(cuts)))
        loudness = loudness * jnp.repeat(draws, shape[dim] // blocks).reshape([-1 if axis == dim else 1 for axis in range(len(shape))])
    return loudness


def bell_draw(own_key, dims, deviation, limit, cuts=(), kind=jnp.bfloat16):
    factor_of = steps_of(own_key, dims, cuts, -0.22, 0.18) if cuts else 1.0
    drawn = jax.random.normal(own_key, dims, jnp.float32) * deviation * factor_of
    return jnp.minimum(jnp.maximum(drawn, -limit), limit).astype(kind)


def setup_inputs(seed: int = 0, part: int = 0) -> dict:
    seeds = jax.random.split(jax.random.key(seed), 10)
    own_keys = jax.random.split(jax.random.fold_in(seeds[9], part), 10)
    currents = bell_draw(own_keys[0], (BOXES, 2, M), 1.0, 6.0, ((0, 16),))
    near_blocks = bell_draw(seeds[1], (BOXES, NB, 2, M, M), (2 * NB * M) ** -0.5, 0.1875, ((0, 16),))
    near_off = draw_near_off(jax.random.fold_in(seeds[9], 71), part)
    radiation = bell_draw(seeds[3], (BOXES, 2, Q, M), (2 * M) ** -0.5, 0.375, ((0, 16),))
    interp = bell_draw(seeds[4], (P_SIZE, Q), Q ** -0.5, 0.5)
    translators = bell_draw(seeds[5], (NT, 2, P_SIZE), (2 * K) ** -0.5, 0.3125, (), jnp.float32)
    send_list = touch_ends(jax.random.randint(seeds[6], (N_BOX, N_BOX, CAP), 0, BOX_DEV), jax.random.fold_in(seeds[6], 1), 0, BOX_DEV - 1).astype(jnp.int32)
    inter_slot = draw_inter_slot(jax.random.fold_in(seeds[9], 71), part)
    trans_id = touch_ends(jax.random.randint(seeds[8], (BOXES, K), 0, NT), jax.random.fold_in(seeds[8], 1), 0, NT - 1).astype(jnp.int32)
    return dict(currents=currents, near_blocks=near_blocks, near_off=near_off, radiation=radiation, interp=interp, translators=translators, send_list=send_list, inter_slot=inter_slot, trans_id=trans_id)


def reference(currents, near_blocks, near_off, radiation, interp, translators, send_list, inter_slot, trans_id):
    peer_count = BOXES // BOX_DEV
    rim_width = BOX_DEV // 2
    values = currents.astype(jnp.float32)
    padded = jnp.pad(values, ((rim_width, rim_width), (0, 0), (0, 0)))
    box_index = jnp.arange(BOXES, dtype=jnp.int32)
    near_field = jnp.zeros((BOXES, 2, M), jnp.float32)
    for entry in range(NB):
        sources = padded[box_index + rim_width + near_off[:, entry].astype(jnp.int32)]
        blocks = near_blocks[:, entry].astype(jnp.float32)
        parts = jnp.einsum("bcij,bej->bcei", blocks, sources)
        near_field = near_field + jnp.stack([parts[:, 0, 0] - parts[:, 1, 1], parts[:, 0, 1] + parts[:, 1, 0]], axis=1)
    rad_float = radiation.astype(jnp.float32)
    parts = jnp.einsum("bcqm,bem->bceq", rad_float, values)
    coarse = jnp.stack([parts[:, 0, 0] - parts[:, 1, 1], parts[:, 0, 1] + parts[:, 1, 0]], axis=1).astype(jnp.bfloat16)
    interp_float = interp.astype(jnp.float32)
    pattern = jnp.einsum("pq,bcq->bcp", interp_float, coarse.astype(jnp.float32)).astype(jnp.bfloat16)
    senders = jnp.arange(peer_count, dtype=jnp.int32) * BOX_DEV
    table = (jnp.transpose(send_list, (1, 0, 2)).astype(jnp.int32) + senders[None, :, None]).reshape(peer_count, peer_count * CAP)
    owners = box_index // BOX_DEV
    partners = table[owners[:, None], inter_slot.astype(jnp.int32)]

    def translate(total, column):
        box_ids, kinds = column
        pats = pattern[box_ids].astype(jnp.float32)
        shifts = translators[kinds]
        real_part = shifts[:, 0] * pats[:, 0] - shifts[:, 1] * pats[:, 1]
        imag_part = shifts[:, 0] * pats[:, 1] + shifts[:, 1] * pats[:, 0]
        return total + jnp.stack([real_part, imag_part], axis=1), None

    start = jnp.zeros((BOXES, 2, P_SIZE), jnp.float32)
    incoming, unused = lax.scan(translate, start, (partners.T, trans_id.astype(jnp.int32).T))
    incoming = incoming.astype(jnp.bfloat16)
    coarse_in = jnp.einsum("pq,bcp->bcq", interp_float, incoming.astype(jnp.float32)).astype(jnp.bfloat16)
    parts = jnp.einsum("bcqm,beq->bcem", rad_float, coarse_in.astype(jnp.float32))
    far_field = jnp.stack([parts[:, 0, 0] + parts[:, 1, 1], parts[:, 0, 1] - parts[:, 1, 0]], axis=1)
    return (near_field + far_field).astype(jnp.bfloat16)
```

```python
import functools

import jax
import jax.numpy as jnp
from jax import lax
from jax.experimental import pallas as pl
from jax.experimental.pallas import tpu as pltpu
from jax.sharding import PartitionSpec as P

reach = 3
span = 2 * reach + 1
rows_box = 8
lane = 128
half, full = jnp.bfloat16, jnp.float32


def dot(a, b):
    return lax.dot_general(a, b, (((1,), (0,)), ((), ())), preferred_element_type=full)


def dot_t(a, b):
    return lax.dot_general(a, b, (((1,), (1,)), ((), ())), preferred_element_type=full)


def iota(shape, dim):
    return lax.broadcasted_iota(jnp.int32, shape, dim)


def one_hot(condition):
    return jnp.where(condition, 1.0, 0.0).astype(half)


def turned(value):
    count = value.shape[0]
    even = (iota(value.shape, 0) & 1) == 0
    return jnp.where(even, -pltpu.roll(value, count - 1, 0), pltpu.roll(value, 1, 0))


def kernel(
    groups, peers, near_chunks, rad_chunks, batch,
    cur_ref, near_hbm, off_ref, rad_hbm, interp_ref, trans_hbm, list_ref, slot_ref, kind_ref,
    out_ref,
    near, rad, trans, table, src, near_sum, far_sum, spread, coarse_sum, outgoing, arrived,
    counts, pats, slots, kinds, inc, back, stage, result,
    near_sem, rad_sem, trans_sem, cur_send, cur_recv, pat_send, pat_recv, res_send, res_recv,
):
    group, place = lax.axis_index("groups"), lax.axis_index("box")
    boxes = rad.shape[0]
    mine = near.shape[0]
    rim = boxes // 2
    cap = outgoing.shape[2]
    first = group * mine
    samples = interp_ref.shape[0]
    blocks = samples // lane
    entries = slot_ref.shape[1]
    table_rows = table.shape[1]

    def device(shift, turn):
        return (lax.rem(group + turn, groups), lax.rem(place + shift + peers, peers))

    others = [
        (shift, turn)
        for turn in range(groups)
        for shift in range(-reach, reach + 1)
        if (shift, turn) != (0, 0)
    ]
    barrier = pltpu.get_barrier_semaphore()
    for shift, turn in others:
        pl.semaphore_signal(
            barrier, inc=1, device_id=device(shift, turn), device_id_type=pl.DeviceIdType.MESH
        )

    rad_step, near_step = boxes // rad_chunks, mine // near_chunks
    rad_copies = [
        pltpu.make_async_copy(
            rad_hbm.at[pl.ds(q * rad_step, rad_step)],
            rad.at[pl.ds(q * rad_step, rad_step)],
            rad_sem.at[q],
        )
        for q in range(rad_chunks)
    ]
    near_copies = [
        pltpu.make_async_copy(
            near_hbm.at[pl.ds(first + q * near_step, near_step)],
            near.at[pl.ds(q * near_step, near_step)],
            near_sem.at[q],
        )
        for q in range(near_chunks)
    ]
    trans_copy = pltpu.make_async_copy(trans_hbm, trans, trans_sem)
    for copy in rad_copies + [trans_copy] + near_copies:
        copy.start()

    pl.semaphore_wait(barrier, len(others))

    inner = 2 * boxes
    edge = 2 * rim
    parts = {
        1: (pl.ds(inner - edge, edge), pl.ds(0, edge)),
        0: (pl.ds(0, inner), pl.ds(edge, inner)),
        -1: (pl.ds(0, edge), pl.ds(edge + inner, edge)),
    }
    cur_copies = []
    for turn in range(groups):
        seen = (groups - turn) % groups
        for shift in (1, -1, 0):
            if (shift, turn) == (0, 0):
                continue
            source, target = parts[shift]
            copy = pltpu.make_async_remote_copy(
                src_ref=cur_ref.at[source],
                dst_ref=table.at[seen, target],
                send_sem=cur_send.at[shift + 1, turn],
                recv_sem=cur_recv.at[shift + 1, seen],
                device_id=device(shift, turn),
                device_id_type=pl.DeviceIdType.MESH,
            )
            copy.start()
            cur_copies.append(copy)
    table[0, pl.ds(edge, inner), :] = cur_ref[...]

    row = iota((boxes * rows_box, inner), 0)
    column = iota((boxes * rows_box, inner), 1)
    wanted = ((row >> 3) << 1) + (row & 7)
    spread[...] = dot(one_hot((column == wanted) & ((row & 7) < 2)), cur_ref[...])

    def coarse_step(step, carry):
        for i in range(4):
            box = step * 4 + i
            at = pl.ds(pl.multiple_of(box * rows_box, rows_box), rows_box)
            coarse_sum[at, :] = dot_t(
                spread[at, :].astype(half), rad[box].reshape(2 * lane, lane)
            )
        return carry

    for q in range(rad_chunks):
        rad_copies[q].wait()
        lax.fori_loop(q * rad_step // 4, (q + 1) * rad_step // 4, coarse_step, 0)
    coarse = (coarse_sum[:, :lane] + turned(coarse_sum[:, lane:])).astype(half)

    count = span * 2 * cap
    per = 2 * cap
    row = iota((count, peers), 0)
    target = lax.rem(place + row // per - reach + peers, peers)
    listed = dot(one_hot(iota((count, peers), 1) == target), list_ref[...].astype(full).astype(half))
    row = iota((count, cap), 0)
    listed = jnp.sum(
        jnp.where(iota((count, cap), 1) == row % cap, listed, 0.0), axis=1, keepdims=True
    )
    row = iota((count, 1), 0)
    listed = listed.astype(jnp.int32) * rows_box + (row % per) // cap
    chosen = dot(one_hot(iota((count, boxes * rows_box), 1) == listed), coarse)
    outgoing[...] = chosen.astype(half).reshape(outgoing.shape)
    pat_copies = []
    for shift, turn in others:
        seen = (groups - turn) % groups
        copy = pltpu.make_async_remote_copy(
            src_ref=outgoing.at[shift + reach],
            dst_ref=arrived.at[seen, reach - shift],
            send_sem=pat_send.at[turn, shift + reach],
            recv_sem=pat_recv.at[seen, reach - shift],
            device_id=device(shift, turn),
            device_id_type=pl.DeviceIdType.MESH,
        )
        copy.start()
        pat_copies.append(copy)
    arrived[0, reach] = outgoing[reach]

    slots[...] = jnp.full(slots.shape, -1, jnp.int32)
    kinds[...] = jnp.full(kinds.shape, -1, jnp.int32)
    own_rows = pl.ds(pl.multiple_of(first, 8), mine)
    slots[:, :entries] = slot_ref[own_rows, :] - (place - reach) * cap
    kinds[:, :entries] = kind_ref[own_rows, :]
    live, kind_rows = counts.shape[1], counts.shape[2]

    def count_step(step, carry):
        for i in range(2):
            box = step * 2 + i
            slot_row = slots[pl.ds(box, 1), :]
            kind_row = kinds[pl.ds(box, 1), :]
            wide = slots.shape[1]
            by_slot = one_hot(iota((live, wide), 0) == slot_row)
            by_kind = one_hot(iota((kind_rows, wide), 0) == kind_row)
            counts[box] = dot_t(by_slot, by_kind).astype(half)
        return carry

    lax.fori_loop(0, mine // 2, count_step, 0)

    for copy in cur_copies:
        copy.wait()
    row = iota((mine * rows_box, mine), 0)
    moves = dot(
        one_hot(iota((mine * rows_box, mine), 1) == (row >> 3)),
        off_ref[own_rows, :].astype(full).astype(half),
    ).astype(jnp.int32)
    row = iota((mine * rows_box, 1), 0)
    turn, part = (row & 7) >> 1, row & 1
    flat = table[...].reshape(groups * table_rows, lane)
    near_count = moves.shape[1]
    for n in range(near_count):
        position = first + (row >> 3) + moves[:, n : n + 1]
        whole = place * boxes + position
        valid = (whole >= 0) & (whole < peers * boxes) & (turn < groups)
        index = jnp.where(valid, turn * table_rows + (position + rim) * 2 + part, -1)
        picked = one_hot(iota((mine * rows_box, groups * table_rows), 1) == index)
        src[:, n * lane : (n + 1) * lane] = dot(picked, flat)

    def near_step_of(box, carry):
        at = pl.ds(pl.multiple_of(box * rows_box, rows_box), rows_box)
        block = jnp.concatenate(
            [near[box, n].reshape(2 * lane, lane) for n in range(near_count)], axis=1
        )
        near_sum[at, :] = dot_t(src[at, :].astype(half), block)
        return carry

    for q in range(near_chunks):
        near_copies[q].wait()
        lax.fori_loop(q * near_step, (q + 1) * near_step, near_step_of, 0, unroll=2)

    for copy in pat_copies:
        copy.wait()
    for turn in range(groups):
        for part in range(2):
            got = arrived[turn, :, part].reshape(live, lane)
            pats[turn, part] = dot_t(got, interp_ref[...]).astype(half).astype(full)

    trans_copy.wait()
    for j in range(blocks):
        lanes = slice(j * lane, (j + 1) * lane)

        def translate(step, carry):
            start = step * batch
            mixed = dot(
                counts[pl.ds(start, batch)].reshape(batch * live, kind_rows), trans[j]
            ).reshape(batch, live, 2 * lane)
            for i in range(batch):
                real, imag = mixed[i, :, :lane], mixed[i, :, lane:]
                sums = []
                for turn in range(groups):
                    pat_real, pat_imag = pats[turn, 0, :, lanes], pats[turn, 1, :, lanes]
                    sums.append(
                        jnp.sum(real * pat_real - imag * pat_imag, axis=0, keepdims=True)
                    )
                    sums.append(
                        jnp.sum(real * pat_imag + imag * pat_real, axis=0, keepdims=True)
                    )
                if len(sums) < rows_box:
                    sums.append(jnp.zeros((rows_box - len(sums), lane), full))
                at = pl.ds(pl.multiple_of((start + i) * rows_box, rows_box), rows_box)
                inc[at, lanes] = jnp.concatenate(sums, axis=0)
            return carry

        lax.fori_loop(0, mine // batch, translate, 0)

    back[...] = dot(inc[...].astype(half), interp_ref[...])

    def far_step(step, carry):
        for i in range(4):
            box = step * 4 + i
            at = pl.ds(pl.multiple_of(box * rows_box, rows_box), rows_box)
            block = jnp.concatenate([rad[first + box, 0], rad[first + box, 1]], axis=1)
            far_sum[at, :] = dot(back[at, :].astype(half), block)
        return carry

    lax.fori_loop(0, mine // 4, far_step, 0)
    total = (
        near_sum[:, :lane]
        + far_sum[:, :lane]
        + turned(near_sum[:, lane:] - far_sum[:, lane:])
    ).astype(half)
    row = iota((2 * mine, mine * rows_box), 0)
    column = iota((2 * mine, mine * rows_box), 1)
    for turn in range(groups):
        picked = one_hot(column == (row >> 1) * rows_box + 2 * turn + (row & 1))
        stage[turn] = dot(picked, total).astype(half)
    res_copies = []
    for turn in range(1, groups):
        copy = pltpu.make_async_remote_copy(
            src_ref=stage.at[turn],
            dst_ref=result.at[group],
            send_sem=res_send.at[turn],
            recv_sem=res_recv.at[groups - turn],
            device_id=device(0, turn),
            device_id_type=pl.DeviceIdType.MESH,
        )
        copy.start()
        res_copies.append(copy)
    result[group] = stage[0]
    for copy in res_copies:
        copy.wait()
    out_ref[...] = result[...].reshape(out_ref.shape)


def on_device(
    currents, near_blocks, near_off, radiation, interp, translators, send_list, inter_slot, trans_id
):
    groups, peers = lax.axis_size("groups"), lax.axis_size("box")
    boxes, size = currents.shape[0], currents.shape[2]
    mine = boxes // groups
    samples, cap = interp.shape[0], send_list.shape[2]
    blocks = samples // lane
    kind_count = translators.shape[0]
    kind_rows = -(-kind_count // lane) * lane
    wide = -(-inter_slot.shape[1] // lane) * lane
    live = span * cap
    near_count = near_off.shape[1]
    tiles = jnp.transpose(
        translators.astype(half).reshape(kind_count, 2, blocks, lane), (2, 0, 1, 3)
    ).reshape(blocks, kind_count, 2 * lane)
    tiles = jnp.pad(tiles, ((0, 0), (0, kind_rows - kind_count), (0, 0)))
    near_chunks, rad_chunks = 4, 4
    inside = pl.BlockSpec(memory_space=pltpu.VMEM)
    outside = pl.BlockSpec(memory_space=pl.ANY)
    out = pl.pallas_call(
        functools.partial(kernel, groups, peers, near_chunks, rad_chunks, 4),
        out_shape=jax.ShapeDtypeStruct((2 * boxes, size), half),
        in_specs=[inside, outside, inside, outside, inside, outside, inside, inside, inside],
        out_specs=inside,
        scratch_shapes=[
            pltpu.VMEM((mine,) + near_blocks.shape[1:], half),
            pltpu.VMEM(radiation.shape, half),
            pltpu.VMEM(tiles.shape, half),
            pltpu.VMEM((groups, 4 * boxes, size), half),
            pltpu.VMEM((mine * rows_box, near_count * size), full),
            pltpu.VMEM((mine * rows_box, 2 * size), full),
            pltpu.VMEM((mine * rows_box, 2 * size), full),
            pltpu.VMEM((boxes * rows_box, size), full),
            pltpu.VMEM((boxes * rows_box, 2 * size), full),
            pltpu.VMEM((span, 2, cap, lane), half),
            pltpu.VMEM((groups, span, 2, cap, lane), half),
            pltpu.VMEM((mine, live, kind_rows), half),
            pltpu.VMEM((groups, 2, live, samples), full),
            pltpu.VMEM((mine, wide), jnp.int32),
            pltpu.VMEM((mine, wide), jnp.int32),
            pltpu.VMEM((mine * rows_box, samples), full),
            pltpu.VMEM((mine * rows_box, lane), full),
            pltpu.VMEM((groups, 2 * mine, size), half),
            pltpu.VMEM((groups, 2 * mine, size), half),
            pltpu.SemaphoreType.DMA((near_chunks,)),
            pltpu.SemaphoreType.DMA((rad_chunks,)),
            pltpu.SemaphoreType.DMA,
            pltpu.SemaphoreType.DMA((3, groups)),
            pltpu.SemaphoreType.DMA((3, groups)),
            pltpu.SemaphoreType.DMA((groups, span)),
            pltpu.SemaphoreType.DMA((groups, span)),
            pltpu.SemaphoreType.DMA((groups,)),
            pltpu.SemaphoreType.DMA((groups,)),
        ],
        compiler_params=pltpu.CompilerParams(
            collective_id=0, has_side_effects=True, vmem_limit_bytes=50 * 2**20
        ),
    )(
        currents.reshape(2 * boxes, size), near_blocks, near_off, radiation, interp, tiles,
        send_list.reshape(send_list.shape[1:]), inter_slot, trans_id,
    )
    return out.reshape(currents.shape)


def solution(mesh):
    return jax.shard_map(
        on_device,
        mesh=mesh,
        in_specs=(
            P(("groups", "box"), None, None),
            P("box", None, None, None, None),
            P("box", None),
            P("box", None, None, None),
            P(),
            P(),
            P("box", None, None),
            P("box", None),
            P("box", None),
        ),
        out_specs=P(("groups", "box"), None, None),
        check_vma=False,
    )
```

```python
import functools

import jax
import jax.numpy as jnp
from jax import lax
from jax.experimental import pallas as pl
from jax.experimental.pallas import tpu as pltpu
from jax.sharding import PartitionSpec as P

reach = 3
span = 2 * reach + 1
rows_box = 8
lane = 128
half, full = jnp.bfloat16, jnp.float32


def dot(a, b):
    return lax.dot_general(a, b, (((1,), (0,)), ((), ())), preferred_element_type=full)


def dot_t(a, b):
    return lax.dot_general(a, b, (((1,), (1,)), ((), ())), preferred_element_type=full)


def iota(shape, dim):
    return lax.broadcasted_iota(jnp.int32, shape, dim)


def one_hot(condition):
    return jnp.where(condition, 1.0, 0.0).astype(half)


def turned(value):
    count = value.shape[0]
    even = (iota(value.shape, 0) & 1) == 0
    return jnp.where(even, -pltpu.roll(value, count - 1, 0), pltpu.roll(value, 1, 0))


def kernel(
    groups, peers, near_chunks, rad_chunks, batch,
    cur_ref, near_hbm, off_ref, rad_hbm, interp_ref, trans_hbm, list_ref, slot_ref, kind_ref,
    out_ref,
    near, rad, raw, trans, table, src, near_sum, far_sum, spread, coarse_sum, outgoing, arrived,
    counts, marks, mixed_even, mixed_odd, pats, slots, kinds, inc, back, stage, result,
    near_sem, rad_sem, trans_sem, cur_send, cur_recv, pat_send, pat_recv, res_send, res_recv,
):
    group, place = lax.axis_index("groups"), lax.axis_index("box")
    boxes = rad.shape[0]
    mine = near.shape[0]
    rim = boxes // 2
    cap = outgoing.shape[2]
    first = group * mine
    samples = interp_ref.shape[0]
    blocks = samples // lane
    entries = slot_ref.shape[1]
    table_rows = table.shape[1]

    def device(shift, turn):
        return (lax.rem(group + turn, groups), lax.rem(place + shift + peers, peers))

    others = [
        (shift, turn)
        for turn in range(groups)
        for shift in range(-reach, reach + 1)
        if (shift, turn) != (0, 0)
    ]
    barrier = pltpu.get_barrier_semaphore()
    for shift, turn in others:
        pl.semaphore_signal(
            barrier, inc=1, device_id=device(shift, turn), device_id_type=pl.DeviceIdType.MESH
        )

    rad_step, near_step = boxes // rad_chunks, mine // near_chunks
    rad_copies = [
        pltpu.make_async_copy(
            rad_hbm.at[pl.ds(q * rad_step, rad_step)],
            rad.at[pl.ds(q * rad_step, rad_step)],
            rad_sem.at[q],
        )
        for q in range(rad_chunks)
    ]
    near_copies = [
        pltpu.make_async_copy(
            near_hbm.at[pl.ds(first + q * near_step, near_step)],
            near.at[pl.ds(q * near_step, near_step)],
            near_sem.at[q],
        )
        for q in range(near_chunks)
    ]
    trans_copy = pltpu.make_async_copy(trans_hbm, raw, trans_sem)
    for copy in rad_copies + [trans_copy] + near_copies:
        copy.start()

    live, kind_rows = counts.shape[1], counts.shape[2]
    wide = slots.shape[1]
    marks[...] = (iota(marks.shape, 0) - lane).astype(full).astype(half)
    slots[...] = jnp.full(slots.shape, -1.0 - lane, full)
    kinds[...] = jnp.full(kinds.shape, -1.0 - lane, full)
    own_rows = pl.ds(pl.multiple_of(first, 8), mine)
    slots[:, :entries] = (slot_ref[own_rows, :] - (place - reach) * cap - lane).astype(full)
    kinds[:, :entries] = (kind_ref[own_rows, :] - lane).astype(full)
    one, none = jnp.ones((), half), jnp.zeros((), half)

    def matches(numbers, box, rows):
        line = jnp.broadcast_to(numbers[pl.ds(box, 1), :], (16, wide)).astype(half)
        line = jnp.broadcast_to(line[None], (rows // 16, 16, wide)).reshape(rows, wide)
        return jnp.where(marks[:rows, :] == line, one, none)

    def count_step(step, carry):
        for i in range(4):
            box = step * 4 + i
            counts[box] = dot_t(
                matches(slots, box, live), matches(kinds, box, kind_rows)
            ).astype(half)
        return carry

    lax.fori_loop(0, mine // 4, count_step, 0)

    pl.semaphore_wait(barrier, len(others))

    inner = 2 * boxes
    edge = 2 * rim
    parts = {
        1: (pl.ds(inner - edge, edge), pl.ds(0, edge)),
        0: (pl.ds(0, inner), pl.ds(edge, inner)),
        -1: (pl.ds(0, edge), pl.ds(edge + inner, edge)),
    }
    cur_copies = []
    for turn in range(groups):
        seen = (groups - turn) % groups
        for shift in (1, -1, 0):
            if (shift, turn) == (0, 0):
                continue
            source, target = parts[shift]
            copy = pltpu.make_async_remote_copy(
                src_ref=cur_ref.at[source],
                dst_ref=table.at[seen, target],
                send_sem=cur_send.at[shift + 1, turn],
                recv_sem=cur_recv.at[shift + 1, seen],
                device_id=device(shift, turn),
                device_id_type=pl.DeviceIdType.MESH,
            )
            copy.start()
            cur_copies.append(copy)
    table[0, pl.ds(edge, inner), :] = cur_ref[...]

    row = iota((boxes * rows_box, inner), 0)
    column = iota((boxes * rows_box, inner), 1)
    wanted = ((row >> 3) << 1) + (row & 7)
    spread[...] = dot(one_hot((column == wanted) & ((row & 7) < 2)), cur_ref[...])

    def coarse_step(step, carry):
        for i in range(4):
            box = step * 4 + i
            at = pl.ds(pl.multiple_of(box * rows_box, rows_box), rows_box)
            coarse_sum[at, :] = dot_t(
                spread[at, :].astype(half), rad[box].reshape(2 * lane, lane)
            )
        return carry

    for q in range(rad_chunks):
        rad_copies[q].wait()
        lax.fori_loop(q * rad_step // 4, (q + 1) * rad_step // 4, coarse_step, 0)
    coarse = (coarse_sum[:, :lane] + turned(coarse_sum[:, lane:])).astype(half)

    count = span * 2 * cap
    per = 2 * cap
    row = iota((count, peers), 0)
    target = lax.rem(place + row // per - reach + peers, peers)
    listed = dot(one_hot(iota((count, peers), 1) == target), list_ref[...].astype(full).astype(half))
    row = iota((count, cap), 0)
    listed = jnp.sum(
        jnp.where(iota((count, cap), 1) == row % cap, listed, 0.0), axis=1, keepdims=True
    )
    row = iota((count, 1), 0)
    listed = listed.astype(jnp.int32) * rows_box + (row % per) // cap
    chosen = dot(one_hot(iota((count, boxes * rows_box), 1) == listed), coarse)
    outgoing[...] = chosen.astype(half).reshape(outgoing.shape)
    pat_copies = []
    for shift, turn in others:
        seen = (groups - turn) % groups
        copy = pltpu.make_async_remote_copy(
            src_ref=outgoing.at[shift + reach],
            dst_ref=arrived.at[seen, reach - shift],
            send_sem=pat_send.at[turn, shift + reach],
            recv_sem=pat_recv.at[seen, reach - shift],
            device_id=device(shift, turn),
            device_id_type=pl.DeviceIdType.MESH,
        )
        copy.start()
        pat_copies.append(copy)
    arrived[0, reach] = outgoing[reach]

    for copy in cur_copies:
        copy.wait()
    row = iota((mine * rows_box, boxes), 0)
    moves = dot_t(
        one_hot(iota((mine * rows_box, boxes), 1) == first + (row >> 3)),
        off_ref[...].astype(full).astype(half),
    ).astype(jnp.int32)
    row = iota((mine * rows_box, 1), 0)
    turn, part = (row & 7) >> 1, row & 1
    flat = table[...].reshape(groups * table_rows, lane)
    near_count = moves.shape[1]
    for n in range(near_count):
        position = first + (row >> 3) + moves[:, n : n + 1]
        whole = place * boxes + position
        valid = (whole >= 0) & (whole < peers * boxes) & (turn < groups)
        index = jnp.where(valid, turn * table_rows + (position + rim) * 2 + part, -1)
        picked = one_hot(iota((mine * rows_box, groups * table_rows), 1) == index)
        src[:, n * lane : (n + 1) * lane] = dot(picked, flat)

    def near_step_of(box, carry):
        at = pl.ds(pl.multiple_of(box * rows_box, rows_box), rows_box)
        block = jnp.concatenate(
            [near[box, n].reshape(2 * lane, lane) for n in range(near_count)], axis=1
        )
        near_sum[at, :] = dot_t(src[at, :].astype(half), block)
        return carry

    for q in range(near_chunks):
        near_copies[q].wait()
        lax.fori_loop(q * near_step, (q + 1) * near_step, near_step_of, 0, unroll=4)

    trans_copy.wait()
    kind_count = raw.shape[0] // (2 * blocks)
    whole_rows = -(-kind_count // 16) * 16
    for j in range(blocks):
        for part in range(2):
            piece = raw[pl.ds(j * 2 + part, kind_count, stride=2 * blocks), :]
            if whole_rows > kind_count:
                piece = jnp.concatenate(
                    [piece, jnp.zeros((whole_rows - kind_count, lane), full)], axis=0
                )
            trans[j, :whole_rows, part * lane : (part + 1) * lane] = piece.astype(half)
        if kind_rows > whole_rows:
            trans[j, whole_rows:, :] = jnp.zeros((kind_rows - whole_rows, 2 * lane), half)

    for copy in pat_copies:
        copy.wait()
    for turn in range(groups):
        for part in range(2):
            got = arrived[turn, :, part].reshape(live, lane)
            pattern = dot_t(got, interp_ref[...]).astype(half).astype(full)
            for j in range(blocks):
                pats[j, turn, part] = pattern[:, j * lane : (j + 1) * lane]

    chunks = mine // batch
    steps = blocks * chunks

    def mix(step, into):
        j, chunk = step // chunks, lax.rem(step, chunks)
        into[...] = dot(
            counts[pl.ds(chunk * batch, batch)].reshape(batch * live, kind_rows), trans[j]
        )

    def translate(step, mixed):
        j, chunk = step // chunks, lax.rem(step, chunks)
        for i in range(batch):
            rows = slice(i * live, (i + 1) * live)
            real, imag = mixed[rows, :lane], mixed[rows, lane:]
            sums = []
            for turn in range(groups):
                pat_real, pat_imag = pats[j, turn, 0], pats[j, turn, 1]
                sums.append(jnp.sum(real * pat_real - imag * pat_imag, axis=0, keepdims=True))
                sums.append(jnp.sum(real * pat_imag + imag * pat_real, axis=0, keepdims=True))
            if len(sums) < rows_box:
                sums.append(jnp.zeros((rows_box - len(sums), lane), full))
            at = pl.ds(pl.multiple_of((chunk * batch + i) * rows_box, rows_box), rows_box)
            inc[j, at, :] = jnp.concatenate(sums, axis=0)

    def pair(step, carry):
        mix(2 * step + 1, mixed_odd)
        translate(2 * step, mixed_even)
        mix(jnp.minimum(2 * step + 2, steps - 1), mixed_even)
        translate(2 * step + 1, mixed_odd)
        return carry

    mix(0, mixed_even)
    lax.fori_loop(0, steps // 2, pair, 0)

    back[...] = dot(
        jnp.concatenate([inc[j].astype(half) for j in range(blocks)], axis=1), interp_ref[...]
    )

    def far_step(step, carry):
        for i in range(4):
            box = step * 4 + i
            at = pl.ds(pl.multiple_of(box * rows_box, rows_box), rows_box)
            block = jnp.concatenate([rad[first + box, 0], rad[first + box, 1]], axis=1)
            far_sum[at, :] = dot(back[at, :].astype(half), block)
        return carry

    lax.fori_loop(0, mine // 4, far_step, 0)
    total = (
        near_sum[:, :lane]
        + far_sum[:, :lane]
        + turned(near_sum[:, lane:] - far_sum[:, lane:])
    ).astype(half)
    row = iota((2 * mine, mine * rows_box), 0)
    column = iota((2 * mine, mine * rows_box), 1)
    for turn in range(groups):
        picked = one_hot(column == (row >> 1) * rows_box + 2 * turn + (row & 1))
        stage[turn] = dot(picked, total).astype(half)
    res_copies = []
    for turn in range(1, groups):
        copy = pltpu.make_async_remote_copy(
            src_ref=stage.at[turn],
            dst_ref=result.at[group],
            send_sem=res_send.at[turn],
            recv_sem=res_recv.at[groups - turn],
            device_id=device(0, turn),
            device_id_type=pl.DeviceIdType.MESH,
        )
        copy.start()
        res_copies.append(copy)
    result[group] = stage[0]
    for copy in res_copies:
        copy.wait()
    out_ref[...] = result[...].reshape(out_ref.shape)


def on_device(
    currents, near_blocks, near_off, radiation, interp, translators, send_list, inter_slot, trans_id
):
    groups, peers = lax.axis_size("groups"), lax.axis_size("box")
    boxes, size = currents.shape[0], currents.shape[2]
    mine = boxes // groups
    samples, cap = interp.shape[0], send_list.shape[2]
    blocks = samples // lane
    kind_count = translators.shape[0]
    kind_rows = -(-kind_count // lane) * lane
    wide = -(-inter_slot.shape[1] // lane) * lane
    live = span * cap
    near_count = near_off.shape[1]
    tiles = jnp.transpose(
        translators.reshape(kind_count, 2, blocks, lane), (0, 2, 1, 3)
    ).reshape(kind_count * 2 * blocks, lane)
    batch = 4
    near_chunks, rad_chunks = 4, 4
    inside = pl.BlockSpec(memory_space=pltpu.VMEM)
    outside = pl.BlockSpec(memory_space=pl.ANY)
    out = pl.pallas_call(
        functools.partial(kernel, groups, peers, near_chunks, rad_chunks, batch),
        out_shape=jax.ShapeDtypeStruct((2 * boxes, size), half),
        in_specs=[inside, outside, inside, outside, inside, outside, inside, inside, inside],
        out_specs=inside,
        scratch_shapes=[
            pltpu.VMEM((mine,) + near_blocks.shape[1:], half),
            pltpu.VMEM(radiation.shape, half),
            pltpu.VMEM(tiles.shape, full),
            pltpu.VMEM((blocks, kind_rows, 2 * lane), half),
            pltpu.VMEM((groups, 4 * boxes, size), half),
            pltpu.VMEM((mine * rows_box, near_count * size), full),
            pltpu.VMEM((mine * rows_box, 2 * size), full),
            pltpu.VMEM((mine * rows_box, 2 * size), full),
            pltpu.VMEM((boxes * rows_box, size), full),
            pltpu.VMEM((boxes * rows_box, 2 * size), full),
            pltpu.VMEM((span, 2, cap, lane), half),
            pltpu.VMEM((groups, span, 2, cap, lane), half),
            pltpu.VMEM((mine, live, kind_rows), half),
            pltpu.VMEM((kind_rows, wide), half),
            pltpu.VMEM((batch * live, 2 * lane), full),
            pltpu.VMEM((batch * live, 2 * lane), full),
            pltpu.VMEM((blocks, groups, 2, live, lane), full),
            pltpu.VMEM((mine, wide), full),
            pltpu.VMEM((mine, wide), full),
            pltpu.VMEM((blocks, mine * rows_box, lane), full),
            pltpu.VMEM((mine * rows_box, lane), full),
            pltpu.VMEM((groups, 2 * mine, size), half),
            pltpu.VMEM((groups, 2 * mine, size), half),
            pltpu.SemaphoreType.DMA((near_chunks,)),
            pltpu.SemaphoreType.DMA((rad_chunks,)),
            pltpu.SemaphoreType.DMA,
            pltpu.SemaphoreType.DMA((3, groups)),
            pltpu.SemaphoreType.DMA((3, groups)),
            pltpu.SemaphoreType.DMA((groups, span)),
            pltpu.SemaphoreType.DMA((groups, span)),
            pltpu.SemaphoreType.DMA((groups,)),
            pltpu.SemaphoreType.DMA((groups,)),
        ],
        compiler_params=pltpu.CompilerParams(
            collective_id=0, has_side_effects=True, vmem_limit_bytes=50 * 2**20
        ),
    )(
        currents.reshape(2 * boxes, size), near_blocks, near_off.T, radiation, interp, tiles,
        send_list.reshape(send_list.shape[1:]), inter_slot, trans_id,
    )
    return out.reshape(currents.shape)


def solution(mesh):
    return jax.shard_map(
        on_device,
        mesh=mesh,
        in_specs=(
            P(("groups", "box"), None, None),
            P("box", None, None, None, None),
            P("box", None),
            P("box", None, None, None),
            P(),
            P(),
            P("box", None, None),
            P("box", None),
            P("box", None),
        ),
        out_specs=P(("groups", "box"), None, None),
        check_vma=False,
    )
```

```python
import functools

import jax
import jax.numpy as jnp
from jax import lax
from jax.experimental import pallas as pl
from jax.experimental.pallas import tpu as pltpu
from jax.sharding import PartitionSpec as P

reach = 3
span = 2 * reach + 1
rows_box = 8
lane = 128
half, full = jnp.bfloat16, jnp.float32


def dot(a, b):
    return lax.dot_general(a, b, (((1,), (0,)), ((), ())), preferred_element_type=full)


def dot_t(a, b):
    return lax.dot_general(a, b, (((1,), (1,)), ((), ())), preferred_element_type=full)


def iota(shape, dim):
    return lax.broadcasted_iota(jnp.int32, shape, dim)


def one_hot(condition):
    return jnp.where(condition, 1.0, 0.0).astype(half)


def turned(value):
    count = value.shape[0]
    even = (iota(value.shape, 0) & 1) == 0
    return jnp.where(even, -pltpu.roll(value, count - 1, 0), pltpu.roll(value, 1, 0))


def kernel(
    groups, peers, near_chunks, rad_chunks, batch,
    cur_hbm, near_hbm, off_hbm, rad_hbm, interp_hbm, trans_hbm, list_hbm, slot_hbm, kind_hbm,
    out_ref,
    slot_ref, kind_ref, cur_ref, list_ref, off_ref, interp_ref,
    near, rad, raw, trans, table, src, near_sum, far_sum, spread, coarse_sum, outgoing, arrived,
    counts, marks, mixed_even, mixed_odd, pats, slots, kinds, inc, back, stage, result,
    small_sem, near_sem, rad_sem, trans_sem, cur_send, cur_recv, pat_send, pat_recv, res_send, res_recv,
):
    group, place = lax.axis_index("groups"), lax.axis_index("box")
    boxes = rad.shape[0]
    mine = near.shape[0]
    rim = boxes // 2
    cap = outgoing.shape[2]
    first = group * mine
    samples = interp_ref.shape[0]
    blocks = samples // lane
    entries = slot_ref.shape[1]
    table_rows = table.shape[1]

    def device(shift, turn):
        return (lax.rem(group + turn, groups), lax.rem(place + shift + peers, peers))

    others = [
        (shift, turn)
        for turn in range(groups)
        for shift in range(-reach, reach + 1)
        if (shift, turn) != (0, 0)
    ]
    barrier = pltpu.get_barrier_semaphore()
    for shift, turn in others:
        pl.semaphore_signal(
            barrier, inc=1, device_id=device(shift, turn), device_id_type=pl.DeviceIdType.MESH
        )

    small_copies = [
        pltpu.make_async_copy(source, target, small_sem.at[i])
        for i, (source, target) in enumerate([
            (slot_hbm, slot_ref), (kind_hbm, kind_ref), (cur_hbm, cur_ref),
            (list_hbm, list_ref), (off_hbm, off_ref), (interp_hbm, interp_ref),
        ])
    ]
    rad_step, near_step = boxes // rad_chunks, mine // near_chunks
    rad_copies = [
        pltpu.make_async_copy(
            rad_hbm.at[pl.ds(q * rad_step, rad_step)],
            rad.at[pl.ds(q * rad_step, rad_step)],
            rad_sem.at[q],
        )
        for q in range(rad_chunks)
    ]
    near_copies = [
        pltpu.make_async_copy(
            near_hbm.at[pl.ds(first + q * near_step, near_step)],
            near.at[pl.ds(q * near_step, near_step)],
            near_sem.at[q],
        )
        for q in range(near_chunks)
    ]
    trans_copy = pltpu.make_async_copy(trans_hbm, raw, trans_sem)
    for copy in small_copies + rad_copies + [trans_copy] + near_copies:
        copy.start()

    live, kind_rows = counts.shape[1], counts.shape[2]
    wide = slots.shape[1]
    marks[...] = (iota(marks.shape, 0) - lane).astype(full).astype(half)
    slots[...] = jnp.full(slots.shape, -1.0 - lane, full)
    kinds[...] = jnp.full(kinds.shape, -1.0 - lane, full)
    own_rows = pl.ds(pl.multiple_of(first, 8), mine)
    small_copies[0].wait()
    small_copies[1].wait()
    slots[:, :entries] = (slot_ref[own_rows, :] - (place - reach) * cap - lane).astype(full)
    kinds[:, :entries] = (kind_ref[own_rows, :] - lane).astype(full)
    one, none = jnp.ones((), half), jnp.zeros((), half)

    def matches(numbers, box, rows):
        line = jnp.broadcast_to(numbers[pl.ds(box, 1), :], (16, wide)).astype(half)
        line = jnp.broadcast_to(line[None], (rows // 16, 16, wide)).reshape(rows, wide)
        return jnp.where(marks[:rows, :] == line, one, none)

    def count_step(step, carry):
        for i in range(4):
            box = step * 4 + i
            counts[box] = dot_t(
                matches(slots, box, live), matches(kinds, box, kind_rows)
            ).astype(half)
        return carry

    lax.fori_loop(0, mine // 4, count_step, 0)

    for copy in small_copies[2:]:
        copy.wait()
    pl.semaphore_wait(barrier, len(others))

    inner = 2 * boxes
    edge = 2 * rim
    parts = {
        1: (pl.ds(inner - edge, edge), pl.ds(0, edge)),
        0: (pl.ds(0, inner), pl.ds(edge, inner)),
        -1: (pl.ds(0, edge), pl.ds(edge + inner, edge)),
    }
    cur_copies = []
    for turn in range(groups):
        seen = (groups - turn) % groups
        for shift in (1, -1, 0):
            if (shift, turn) == (0, 0):
                continue
            source, target = parts[shift]
            copy = pltpu.make_async_remote_copy(
                src_ref=cur_ref.at[source],
                dst_ref=table.at[seen, target],
                send_sem=cur_send.at[shift + 1, turn],
                recv_sem=cur_recv.at[shift + 1, seen],
                device_id=device(shift, turn),
                device_id_type=pl.DeviceIdType.MESH,
            )
            copy.start()
            cur_copies.append(copy)
    table[0, pl.ds(edge, inner), :] = cur_ref[...]

    row = iota((boxes * rows_box, inner), 0)
    column = iota((boxes * rows_box, inner), 1)
    wanted = ((row >> 3) << 1) + (row & 7)
    spread[...] = dot(one_hot((column == wanted) & ((row & 7) < 2)), cur_ref[...])

    def coarse_step(step, carry):
        for i in range(4):
            box = step * 4 + i
            at = pl.ds(pl.multiple_of(box * rows_box, rows_box), rows_box)
            coarse_sum[at, :] = dot_t(
                spread[at, :].astype(half), rad[box].reshape(2 * lane, lane)
            )
        return carry

    for q in range(rad_chunks):
        rad_copies[q].wait()
        lax.fori_loop(q * rad_step // 4, (q + 1) * rad_step // 4, coarse_step, 0)
    coarse = (coarse_sum[:, :lane] + turned(coarse_sum[:, lane:])).astype(half)

    count = span * 2 * cap
    per = 2 * cap
    row = iota((count, peers), 0)
    target = lax.rem(place + row // per - reach + peers, peers)
    listed = dot(one_hot(iota((count, peers), 1) == target), list_ref[...].astype(full).astype(half))
    row = iota((count, cap), 0)
    listed = jnp.sum(
        jnp.where(iota((count, cap), 1) == row % cap, listed, 0.0), axis=1, keepdims=True
    )
    row = iota((count, 1), 0)
    listed = listed.astype(jnp.int32) * rows_box + (row % per) // cap
    chosen = dot(one_hot(iota((count, boxes * rows_box), 1) == listed), coarse)
    outgoing[...] = chosen.astype(half).reshape(outgoing.shape)
    pat_copies = []
    for shift, turn in others:
        seen = (groups - turn) % groups
        copy = pltpu.make_async_remote_copy(
            src_ref=outgoing.at[shift + reach],
            dst_ref=arrived.at[seen, reach - shift],
            send_sem=pat_send.at[turn, shift + reach],
            recv_sem=pat_recv.at[seen, reach - shift],
            device_id=device(shift, turn),
            device_id_type=pl.DeviceIdType.MESH,
        )
        copy.start()
        pat_copies.append(copy)
    arrived[0, reach] = outgoing[reach]

    for copy in cur_copies:
        copy.wait()
    row = iota((mine * rows_box, boxes), 0)
    moves = dot_t(
        one_hot(iota((mine * rows_box, boxes), 1) == first + (row >> 3)),
        off_ref[...].astype(full).astype(half),
    ).astype(jnp.int32)
    row = iota((mine * rows_box, 1), 0)
    turn, part = (row & 7) >> 1, row & 1
    flat = table[...].reshape(groups * table_rows, lane)
    near_count = moves.shape[1]
    for n in range(near_count):
        position = first + (row >> 3) + moves[:, n : n + 1]
        whole = place * boxes + position
        valid = (whole >= 0) & (whole < peers * boxes) & (turn < groups)
        index = jnp.where(valid, turn * table_rows + (position + rim) * 2 + part, -1)
        picked = one_hot(iota((mine * rows_box, groups * table_rows), 1) == index)
        src[:, n * lane : (n + 1) * lane] = dot(picked, flat)

    def near_step_of(box, carry):
        at = pl.ds(pl.multiple_of(box * rows_box, rows_box), rows_box)
        block = jnp.concatenate(
            [near[box, n].reshape(2 * lane, lane) for n in range(near_count)], axis=1
        )
        near_sum[at, :] = dot_t(src[at, :].astype(half), block)
        return carry

    for q in range(near_chunks):
        near_copies[q].wait()
        lax.fori_loop(q * near_step, (q + 1) * near_step, near_step_of, 0, unroll=4)

    trans_copy.wait()
    kind_count = raw.shape[0] // (2 * blocks)
    whole_rows = -(-kind_count // 16) * 16
    for j in range(blocks):
        for part in range(2):
            piece = raw[pl.ds(j * 2 + part, kind_count, stride=2 * blocks), :]
            if whole_rows > kind_count:
                piece = jnp.concatenate(
                    [piece, jnp.zeros((whole_rows - kind_count, lane), full)], axis=0
                )
            trans[j, :whole_rows, part * lane : (part + 1) * lane] = piece.astype(half)
        if kind_rows > whole_rows:
            trans[j, whole_rows:, :] = jnp.zeros((kind_rows - whole_rows, 2 * lane), half)

    for copy in pat_copies:
        copy.wait()
    for turn in range(groups):
        for part in range(2):
            got = arrived[turn, :, part].reshape(live, lane)
            pattern = dot_t(got, interp_ref[...]).astype(half).astype(full)
            for j in range(blocks):
                pats[j, turn, part] = pattern[:, j * lane : (j + 1) * lane]

    chunks = mine // batch
    steps = blocks * chunks

    def mix(step, into):
        j, chunk = step // chunks, lax.rem(step, chunks)
        into[...] = dot(
            counts[pl.ds(chunk * batch, batch)].reshape(batch * live, kind_rows), trans[j]
        )

    def translate(step, mixed):
        j, chunk = step // chunks, lax.rem(step, chunks)
        for i in range(batch):
            rows = slice(i * live, (i + 1) * live)
            real, imag = mixed[rows, :lane], mixed[rows, lane:]
            sums = []
            for turn in range(groups):
                pat_real, pat_imag = pats[j, turn, 0], pats[j, turn, 1]
                sums.append(jnp.sum(real * pat_real - imag * pat_imag, axis=0, keepdims=True))
                sums.append(jnp.sum(real * pat_imag + imag * pat_real, axis=0, keepdims=True))
            if len(sums) < rows_box:
                sums.append(jnp.zeros((rows_box - len(sums), lane), full))
            at = pl.ds(pl.multiple_of((chunk * batch + i) * rows_box, rows_box), rows_box)
            inc[j, at, :] = jnp.concatenate(sums, axis=0)

    def pair(step, carry):
        mix(2 * step + 1, mixed_odd)
        translate(2 * step, mixed_even)
        mix(jnp.minimum(2 * step + 2, steps - 1), mixed_even)
        translate(2 * step + 1, mixed_odd)
        return carry

    mix(0, mixed_even)
    lax.fori_loop(0, steps // 2, pair, 0)

    back[...] = dot(
        jnp.concatenate([inc[j].astype(half) for j in range(blocks)], axis=1), interp_ref[...]
    )

    def far_step(step, carry):
        for i in range(4):
            box = step * 4 + i
            at = pl.ds(pl.multiple_of(box * rows_box, rows_box), rows_box)
            block = jnp.concatenate([rad[first + box, 0], rad[first + box, 1]], axis=1)
            far_sum[at, :] = dot(back[at, :].astype(half), block)
        return carry

    lax.fori_loop(0, mine // 4, far_step, 0)
    total = (
        near_sum[:, :lane]
        + far_sum[:, :lane]
        + turned(near_sum[:, lane:] - far_sum[:, lane:])
    ).astype(half)
    row = iota((2 * mine, mine * rows_box), 0)
    column = iota((2 * mine, mine * rows_box), 1)
    for turn in range(groups):
        picked = one_hot(column == (row >> 1) * rows_box + 2 * turn + (row & 1))
        stage[turn] = dot(picked, total).astype(half)
    res_copies = []
    for turn in range(1, groups):
        copy = pltpu.make_async_remote_copy(
            src_ref=stage.at[turn],
            dst_ref=result.at[group],
            send_sem=res_send.at[turn],
            recv_sem=res_recv.at[groups - turn],
            device_id=device(0, turn),
            device_id_type=pl.DeviceIdType.MESH,
        )
        copy.start()
        res_copies.append(copy)
    result[group] = stage[0]
    for copy in res_copies:
        copy.wait()
    out_ref[...] = result[...].reshape(out_ref.shape)


def on_device(
    currents, near_blocks, near_off, radiation, interp, translators, send_list, inter_slot, trans_id
):
    groups, peers = lax.axis_size("groups"), lax.axis_size("box")
    boxes, size = currents.shape[0], currents.shape[2]
    mine = boxes // groups
    samples, cap = interp.shape[0], send_list.shape[2]
    blocks = samples // lane
    kind_count = translators.shape[0]
    kind_rows = -(-kind_count // lane) * lane
    wide = -(-inter_slot.shape[1] // lane) * lane
    live = span * cap
    near_count = near_off.shape[1]
    tiles = jnp.transpose(
        translators.reshape(kind_count, 2, blocks, lane), (0, 2, 1, 3)
    ).reshape(kind_count * 2 * blocks, lane)
    batch = 8
    near_chunks, rad_chunks = 4, 4
    inside = pl.BlockSpec(memory_space=pltpu.VMEM)
    outside = pl.BlockSpec(memory_space=pltpu.HBM)
    out = pl.pallas_call(
        functools.partial(kernel, groups, peers, near_chunks, rad_chunks, batch),
        out_shape=jax.ShapeDtypeStruct((2 * boxes, size), half),
        in_specs=[outside] * 9,
        out_specs=inside,
        scratch_shapes=[
            pltpu.VMEM(inter_slot.shape, jnp.int32),
            pltpu.VMEM(trans_id.shape, jnp.int32),
            pltpu.VMEM((2 * boxes, size), half),
            pltpu.VMEM(send_list.shape[1:], jnp.int32),
            pltpu.VMEM((near_count, boxes), jnp.int32),
            pltpu.VMEM(interp.shape, half),
            pltpu.VMEM((mine,) + near_blocks.shape[1:], half),
            pltpu.VMEM(radiation.shape, half),
            pltpu.VMEM(tiles.shape, full),
            pltpu.VMEM((blocks, kind_rows, 2 * lane), half),
            pltpu.VMEM((groups, 4 * boxes, size), half),
            pltpu.VMEM((mine * rows_box, near_count * size), full),
            pltpu.VMEM((mine * rows_box, 2 * size), full),
            pltpu.VMEM((mine * rows_box, 2 * size), full),
            pltpu.VMEM((boxes * rows_box, size), full),
            pltpu.VMEM((boxes * rows_box, 2 * size), full),
            pltpu.VMEM((span, 2, cap, lane), half),
            pltpu.VMEM((groups, span, 2, cap, lane), half),
            pltpu.VMEM((mine, live, kind_rows), half),
            pltpu.VMEM((kind_rows, wide), half),
            pltpu.VMEM((batch * live, 2 * lane), full),
            pltpu.VMEM((batch * live, 2 * lane), full),
            pltpu.VMEM((blocks, groups, 2, live, lane), full),
            pltpu.VMEM((mine, wide), full),
            pltpu.VMEM((mine, wide), full),
            pltpu.VMEM((blocks, mine * rows_box, lane), full),
            pltpu.VMEM((mine * rows_box, lane), full),
            pltpu.VMEM((groups, 2 * mine, size), half),
            pltpu.VMEM((groups, 2 * mine, size), half),
            pltpu.SemaphoreType.DMA((6,)),
            pltpu.SemaphoreType.DMA((near_chunks,)),
            pltpu.SemaphoreType.DMA((rad_chunks,)),
            pltpu.SemaphoreType.DMA,
            pltpu.SemaphoreType.DMA((3, groups)),
            pltpu.SemaphoreType.DMA((3, groups)),
            pltpu.SemaphoreType.DMA((groups, span)),
            pltpu.SemaphoreType.DMA((groups, span)),
            pltpu.SemaphoreType.DMA((groups,)),
            pltpu.SemaphoreType.DMA((groups,)),
        ],
        compiler_params=pltpu.CompilerParams(
            collective_id=0, has_side_effects=True, vmem_limit_bytes=60 * 2**20
        ),
    )(
        currents.reshape(2 * boxes, size), near_blocks, near_off.T, radiation, interp, tiles,
        send_list.reshape(send_list.shape[1:]), inter_slot, trans_id,
    )
    return out.reshape(currents.shape)


def solution(mesh):
    return jax.shard_map(
        on_device,
        mesh=mesh,
        in_specs=(
            P(("groups", "box"), None, None),
            P("box", None, None, None, None),
            P("box", None),
            P("box", None, None, None),
            P(),
            P(),
            P("box", None, None),
            P("box", None),
            P("box", None),
        ),
        out_specs=P(("groups", "box"), None, None),
        check_vma=False,
    )
```

```python
import functools

import jax
import jax.numpy as jnp
from jax import lax
from jax.experimental import pallas as pl
from jax.experimental.pallas import tpu as pltpu
from jax.sharding import PartitionSpec as P

reach = 3
span = 2 * reach + 1
rows_box = 8
lane = 128
half, full = jnp.bfloat16, jnp.float32


def dot(a, b):
    return lax.dot_general(a, b, (((1,), (0,)), ((), ())), preferred_element_type=full)


def dot_t(a, b):
    return lax.dot_general(a, b, (((1,), (1,)), ((), ())), preferred_element_type=full)


def iota(shape, dim):
    return lax.broadcasted_iota(jnp.int32, shape, dim)


def one_hot(condition):
    return jnp.where(condition, 1.0, 0.0).astype(half)


def turned(value):
    count = value.shape[0]
    even = (iota(value.shape, 0) & 1) == 0
    return jnp.where(even, -pltpu.roll(value, count - 1, 0), pltpu.roll(value, 1, 0))


def kernel(
    groups, peers, near_chunks, rad_chunks, batch,
    cur_hbm, near_hbm, off_hbm, rad_hbm, interp_hbm, trans_hbm, list_hbm, slot_hbm, kind_hbm,
    out_ref,
    slot_ref, kind_ref, cur_ref, list_ref, off_ref, interp_ref,
    near, rad, raw, trans, table, src, near_sum, far_sum, spread, coarse_sum, outgoing, arrived,
    counts, marks, mixed_even, mixed_odd, pats, slots, kinds, inc, back, stage, result,
    small_sem, near_sem, rad_sem, trans_sem, cur_send, cur_recv, pat_send, pat_recv, res_send, res_recv,
):
    group, place = lax.axis_index("groups"), lax.axis_index("box")
    boxes = rad.shape[0]
    mine = near.shape[0]
    rim = boxes // 2
    cap = outgoing.shape[2]
    first = group * mine
    samples = interp_ref.shape[0]
    blocks = samples // lane
    entries = slot_ref.shape[1]
    table_rows = table.shape[1]

    def device(shift, turn):
        return (lax.rem(group + turn, groups), lax.rem(place + shift + peers, peers))

    others = [
        (shift, turn)
        for turn in range(groups)
        for shift in range(-reach, reach + 1)
        if (shift, turn) != (0, 0)
    ]
    barrier = pltpu.get_barrier_semaphore()
    for shift, turn in others:
        pl.semaphore_signal(
            barrier, inc=1, device_id=device(shift, turn), device_id_type=pl.DeviceIdType.MESH
        )

    small_copies = [
        pltpu.make_async_copy(source, target, small_sem.at[i])
        for i, (source, target) in enumerate([
            (slot_hbm, slot_ref), (kind_hbm, kind_ref), (cur_hbm, cur_ref),
            (list_hbm, list_ref), (off_hbm, off_ref), (interp_hbm, interp_ref),
        ])
    ]
    rad_step, near_step = boxes // rad_chunks, mine // near_chunks
    rad_copies = [
        pltpu.make_async_copy(
            rad_hbm.at[pl.ds(q * rad_step, rad_step)],
            rad.at[pl.ds(q * rad_step, rad_step)],
            rad_sem.at[q],
        )
        for q in range(rad_chunks)
    ]
    near_copies = [
        pltpu.make_async_copy(
            near_hbm.at[pl.ds(first + q * near_step, near_step)],
            near.at[pl.ds(q * near_step, near_step)],
            near_sem.at[q],
        )
        for q in range(near_chunks)
    ]
    trans_copy = pltpu.make_async_copy(trans_hbm, raw, trans_sem)
    for copy in small_copies + rad_copies + [trans_copy] + near_copies:
        copy.start()

    live, kind_rows = counts.shape[1], counts.shape[2]
    wide = slots.shape[1]
    marks[...] = (iota(marks.shape, 0) - lane).astype(full).astype(half)
    slots[...] = jnp.full(slots.shape, -1.0 - lane, full)
    kinds[...] = jnp.full(kinds.shape, -1.0 - lane, full)
    own_rows = pl.ds(pl.multiple_of(first, 8), mine)
    small_copies[0].wait()
    small_copies[1].wait()
    slots[:, :entries] = (slot_ref[own_rows, :] - (place - reach) * cap - lane).astype(full)
    kinds[:, :entries] = (kind_ref[own_rows, :] - lane).astype(full)
    one, none = jnp.ones((), half), jnp.zeros((), half)

    def matches(numbers, box, rows):
        line = jnp.broadcast_to(numbers[pl.ds(box, 1), :], (16, wide)).astype(half)
        line = jnp.broadcast_to(line[None], (rows // 16, 16, wide)).reshape(rows, wide)
        return jnp.where(marks[:rows, :] == line, one, none)

    def count_step(step, carry):
        for i in range(8):
            box = step * 8 + i
            counts[box] = dot_t(
                matches(slots, box, live), matches(kinds, box, kind_rows)
            ).astype(half)
        return carry

    lax.fori_loop(0, mine // 8, count_step, 0)

    for copy in small_copies[2:]:
        copy.wait()
    pl.semaphore_wait(barrier, len(others))

    inner = 2 * boxes
    edge = 2 * rim
    parts = {
        1: (pl.ds(inner - edge, edge), pl.ds(0, edge)),
        0: (pl.ds(0, inner), pl.ds(edge, inner)),
        -1: (pl.ds(0, edge), pl.ds(edge + inner, edge)),
    }
    cur_copies = []
    for turn in range(groups):
        seen = (groups - turn) % groups
        for shift in (1, -1, 0):
            if (shift, turn) == (0, 0):
                continue
            source, target = parts[shift]
            copy = pltpu.make_async_remote_copy(
                src_ref=cur_ref.at[source],
                dst_ref=table.at[seen, target],
                send_sem=cur_send.at[shift + 1, turn],
                recv_sem=cur_recv.at[shift + 1, seen],
                device_id=device(shift, turn),
                device_id_type=pl.DeviceIdType.MESH,
            )
            copy.start()
            cur_copies.append(copy)
    table[0, pl.ds(edge, inner), :] = cur_ref[...]

    row = iota((boxes * rows_box, inner), 0)
    column = iota((boxes * rows_box, inner), 1)
    wanted = ((row >> 3) << 1) + (row & 7)
    spread[...] = dot(one_hot((column == wanted) & ((row & 7) < 2)), cur_ref[...])

    def coarse_step(step, carry):
        for i in range(8):
            box = step * 8 + i
            at = pl.ds(pl.multiple_of(box * rows_box, rows_box), rows_box)
            coarse_sum[at, :] = dot_t(
                spread[at, :].astype(half), rad[box].reshape(2 * lane, lane)
            )
        return carry

    for q in range(rad_chunks):
        rad_copies[q].wait()
        lax.fori_loop(q * rad_step // 8, (q + 1) * rad_step // 8, coarse_step, 0)
    coarse = (coarse_sum[:, :lane] + turned(coarse_sum[:, lane:])).astype(half)

    count = span * 2 * cap
    per = 2 * cap
    row = iota((count, peers), 0)
    target = lax.rem(place + row // per - reach + peers, peers)
    listed = dot(one_hot(iota((count, peers), 1) == target), list_ref[...].astype(full).astype(half))
    row = iota((count, cap), 0)
    listed = jnp.sum(
        jnp.where(iota((count, cap), 1) == row % cap, listed, 0.0), axis=1, keepdims=True
    )
    row = iota((count, 1), 0)
    listed = listed.astype(jnp.int32) * rows_box + (row % per) // cap
    chosen = dot(one_hot(iota((count, boxes * rows_box), 1) == listed), coarse)
    outgoing[...] = chosen.astype(half).reshape(outgoing.shape)
    pat_copies = []
    for shift, turn in others:
        seen = (groups - turn) % groups
        copy = pltpu.make_async_remote_copy(
            src_ref=outgoing.at[shift + reach],
            dst_ref=arrived.at[seen, reach - shift],
            send_sem=pat_send.at[turn, shift + reach],
            recv_sem=pat_recv.at[seen, reach - shift],
            device_id=device(shift, turn),
            device_id_type=pl.DeviceIdType.MESH,
        )
        copy.start()
        pat_copies.append(copy)
    arrived[0, reach] = outgoing[reach]

    for copy in cur_copies:
        copy.wait()
    row = iota((mine * rows_box, boxes), 0)
    moves = dot_t(
        one_hot(iota((mine * rows_box, boxes), 1) == first + (row >> 3)),
        off_ref[...].astype(full).astype(half),
    ).astype(jnp.int32)
    row = iota((mine * rows_box, 1), 0)
    turn, part = (row & 7) >> 1, row & 1
    flat = table[...].reshape(groups * table_rows, lane)
    near_count = moves.shape[1]
    for n in range(near_count):
        position = first + (row >> 3) + moves[:, n : n + 1]
        whole = place * boxes + position
        valid = (whole >= 0) & (whole < peers * boxes) & (turn < groups)
        index = jnp.where(valid, turn * table_rows + (position + rim) * 2 + part, -1)
        picked = one_hot(iota((mine * rows_box, groups * table_rows), 1) == index)
        src[:, n * lane : (n + 1) * lane] = dot(picked, flat)

    def near_step_of(box, carry):
        at = pl.ds(pl.multiple_of(box * rows_box, rows_box), rows_box)
        block = jnp.concatenate(
            [near[box, n].reshape(2 * lane, lane) for n in range(near_count)], axis=1
        )
        near_sum[at, :] = dot_t(src[at, :].astype(half), block)
        return carry

    for q in range(near_chunks):
        near_copies[q].wait()
        lax.fori_loop(q * near_step, (q + 1) * near_step, near_step_of, 0, unroll=min(8, near_step))

    trans_copy.wait()
    kind_count = raw.shape[0] // (2 * blocks)
    whole_rows = -(-kind_count // 16) * 16
    for j in range(blocks):
        for part in range(2):
            piece = raw[pl.ds(j * 2 + part, kind_count, stride=2 * blocks), :]
            if whole_rows > kind_count:
                piece = jnp.concatenate(
                    [piece, jnp.zeros((whole_rows - kind_count, lane), full)], axis=0
                )
            trans[j, :whole_rows, part * lane : (part + 1) * lane] = piece.astype(half)
        if kind_rows > whole_rows:
            trans[j, whole_rows:, :] = jnp.zeros((kind_rows - whole_rows, 2 * lane), half)

    for copy in pat_copies:
        copy.wait()
    for turn in range(groups):
        for part in range(2):
            got = arrived[turn, :, part].reshape(live, lane)
            pattern = dot_t(got, interp_ref[...]).astype(half).astype(full)
            for j in range(blocks):
                pats[j, turn, part] = pattern[:, j * lane : (j + 1) * lane]

    chunks = mine // batch
    steps = blocks * chunks

    def mix(step, into):
        j, chunk = step // chunks, lax.rem(step, chunks)
        into[...] = dot(
            counts[pl.ds(chunk * batch, batch)].reshape(batch * live, kind_rows), trans[j]
        )

    def translate(step, mixed):
        j, chunk = step // chunks, lax.rem(step, chunks)
        for i in range(batch):
            rows = slice(i * live, (i + 1) * live)
            real, imag = mixed[rows, :lane], mixed[rows, lane:]
            sums = []
            for turn in range(groups):
                pat_real, pat_imag = pats[j, turn, 0], pats[j, turn, 1]
                sums.append(jnp.sum(real * pat_real - imag * pat_imag, axis=0, keepdims=True))
                sums.append(jnp.sum(real * pat_imag + imag * pat_real, axis=0, keepdims=True))
            if len(sums) < rows_box:
                sums.append(jnp.zeros((rows_box - len(sums), lane), full))
            at = pl.ds(pl.multiple_of((chunk * batch + i) * rows_box, rows_box), rows_box)
            inc[j, at, :] = jnp.concatenate(sums, axis=0)

    def pair(step, carry):
        mix(2 * step + 1, mixed_odd)
        translate(2 * step, mixed_even)
        mix(jnp.minimum(2 * step + 2, steps - 1), mixed_even)
        translate(2 * step + 1, mixed_odd)
        return carry

    mix(0, mixed_even)
    lax.fori_loop(0, steps // 2, pair, 0)

    back[...] = dot(
        jnp.concatenate([inc[j].astype(half) for j in range(blocks)], axis=1), interp_ref[...]
    )

    def far_step(step, carry):
        for i in range(8):
            box = step * 8 + i
            at = pl.ds(pl.multiple_of(box * rows_box, rows_box), rows_box)
            block = jnp.concatenate([rad[first + box, 0], rad[first + box, 1]], axis=1)
            far_sum[at, :] = dot(back[at, :].astype(half), block)
        return carry

    lax.fori_loop(0, mine // 8, far_step, 0)
    total = (
        near_sum[:, :lane]
        + far_sum[:, :lane]
        + turned(near_sum[:, lane:] - far_sum[:, lane:])
    ).astype(half)
    row = iota((2 * mine, mine * rows_box), 0)
    column = iota((2 * mine, mine * rows_box), 1)
    for turn in range(groups):
        picked = one_hot(column == (row >> 1) * rows_box + 2 * turn + (row & 1))
        stage[turn] = dot(picked, total).astype(half)
    res_copies = []
    for turn in range(1, groups):
        copy = pltpu.make_async_remote_copy(
            src_ref=stage.at[turn],
            dst_ref=result.at[group],
            send_sem=res_send.at[turn],
            recv_sem=res_recv.at[groups - turn],
            device_id=device(0, turn),
            device_id_type=pl.DeviceIdType.MESH,
        )
        copy.start()
        res_copies.append(copy)
    result[group] = stage[0]
    for copy in res_copies:
        copy.wait()
    out_ref[...] = result[...].reshape(out_ref.shape)


def on_device(
    currents, near_blocks, near_off, radiation, interp, translators, send_list, inter_slot, trans_id
):
    groups, peers = lax.axis_size("groups"), lax.axis_size("box")
    boxes, size = currents.shape[0], currents.shape[2]
    mine = boxes // groups
    samples, cap = interp.shape[0], send_list.shape[2]
    blocks = samples // lane
    kind_count = translators.shape[0]
    kind_rows = -(-kind_count // lane) * lane
    wide = -(-inter_slot.shape[1] // lane) * lane
    live = span * cap
    near_count = near_off.shape[1]
    tiles = jnp.transpose(
        translators.reshape(kind_count, 2, blocks, lane), (0, 2, 1, 3)
    ).reshape(kind_count * 2 * blocks, lane)
    batch = 8
    near_chunks, rad_chunks = 4, 4
    inside = pl.BlockSpec(memory_space=pltpu.VMEM)
    outside = pl.BlockSpec(memory_space=pltpu.HBM)
    out = pl.pallas_call(
        functools.partial(kernel, groups, peers, near_chunks, rad_chunks, batch),
        out_shape=jax.ShapeDtypeStruct((2 * boxes, size), half),
        in_specs=[outside] * 9,
        out_specs=inside,
        scratch_shapes=[
            pltpu.VMEM(inter_slot.shape, jnp.int32),
            pltpu.VMEM(trans_id.shape, jnp.int32),
            pltpu.VMEM((2 * boxes, size), half),
            pltpu.VMEM(send_list.shape[1:], jnp.int32),
            pltpu.VMEM((near_count, boxes), jnp.int32),
            pltpu.VMEM(interp.shape, half),
            pltpu.VMEM((mine,) + near_blocks.shape[1:], half),
            pltpu.VMEM(radiation.shape, half),
            pltpu.VMEM(tiles.shape, full),
            pltpu.VMEM((blocks, kind_rows, 2 * lane), half),
            pltpu.VMEM((groups, 4 * boxes, size), half),
            pltpu.VMEM((mine * rows_box, near_count * size), full),
            pltpu.VMEM((mine * rows_box, 2 * size), full),
            pltpu.VMEM((mine * rows_box, 2 * size), full),
            pltpu.VMEM((boxes * rows_box, size), full),
            pltpu.VMEM((boxes * rows_box, 2 * size), full),
            pltpu.VMEM((span, 2, cap, lane), half),
            pltpu.VMEM((groups, span, 2, cap, lane), half),
            pltpu.VMEM((mine, live, kind_rows), half),
            pltpu.VMEM((kind_rows, wide), half),
            pltpu.VMEM((batch * live, 2 * lane), full),
            pltpu.VMEM((batch * live, 2 * lane), full),
            pltpu.VMEM((blocks, groups, 2, live, lane), full),
            pltpu.VMEM((mine, wide), full),
            pltpu.VMEM((mine, wide), full),
            pltpu.VMEM((blocks, mine * rows_box, lane), full),
            pltpu.VMEM((mine * rows_box, lane), full),
            pltpu.VMEM((groups, 2 * mine, size), half),
            pltpu.VMEM((groups, 2 * mine, size), half),
            pltpu.SemaphoreType.DMA((6,)),
            pltpu.SemaphoreType.DMA((near_chunks,)),
            pltpu.SemaphoreType.DMA((rad_chunks,)),
            pltpu.SemaphoreType.DMA,
            pltpu.SemaphoreType.DMA((3, groups)),
            pltpu.SemaphoreType.DMA((3, groups)),
            pltpu.SemaphoreType.DMA((groups, span)),
            pltpu.SemaphoreType.DMA((groups, span)),
            pltpu.SemaphoreType.DMA((groups,)),
            pltpu.SemaphoreType.DMA((groups,)),
        ],
        compiler_params=pltpu.CompilerParams(
            collective_id=0, has_side_effects=True, vmem_limit_bytes=60 * 2**20
        ),
    )(
        currents.reshape(2 * boxes, size), near_blocks, near_off.T, radiation, interp, tiles,
        send_list.reshape(send_list.shape[1:]), inter_slot, trans_id,
    )
    return out.reshape(currents.shape)


def solution(mesh):
    return jax.shard_map(
        on_device,
        mesh=mesh,
        in_specs=(
            P(("groups", "box"), None, None),
            P("box", None, None, None, None),
            P("box", None),
            P("box", None, None, None),
            P(),
            P(),
            P("box", None, None),
            P("box", None),
            P("box", None),
        ),
        out_specs=P(("groups", "box"), None, None),
        check_vma=False,
    )
```
